32 devices in a mesh: row: 4 (over y, x), col: 8 (over z, core).
Axes of the slice: x: 2, y: 2, z: 4, core: 2. Of those that a mesh axis runs over, the one named last changes fastest.
Arguments:
- forcing: float32 [2, 8, 16, 16384], P(None, None, None, ('row', 'col')), may hold values from -6 to 6
- elem_area: float32 [16384], P(('row', 'col')), may hold values from 0.5 to 2
- send_elem: int32 [4, 64, 128], P('row', 'col'), may hold values from -1 to 511, as said below
- intersection_entry_slot: int32 [4, 8192], P(None, ('row', 'col')), may hold values from -1 to 1023, as said below
- entry_weight: float32 [4, 8192], P(None, ('row', 'col')), may hold values from 0.1 to 1
- entry_coords: float32 [2, 4, 8192], P(None, None, ('row', 'col')), may hold values from -1 to 1
- land_area: float32 [8192], P(('row', 'col')), may hold values from 1 to 4
- soil_temp: float32 [20, 8192], P(None, ('row', 'col')), may hold values from 0.5 to 1.5
- soil_cond: float32 [20, 8192], P(None, ('row', 'col')), may hold values from 0.2 to 2
- heat_cap: float32 [20, 8192], P(None, ('row', 'col')), may hold values from 0.5 to 2
- layer_count: int32 [8192], P(('row', 'col')), may hold values from 8 to 20
- snow_count: int32 [8192], P(('row', 'col')), may hold values from 0 to 5
- mix: float32 [8], replicated, may hold values from 0.3 to 1
Outputs:
- flux_nodes: float32 [2, 4, 16, 16384], P(None, None, None, ('row', 'col'))
- soil_new: float32 [20, 8192], P(None, ('row', 'col'))
The draws below stay inside these ranges and needn't reach their ends.
Inputs may be any that keep to these rules, and one draw needn't show every extreme that they name: `send_elem`: -1 marks an empty slot. Intersections are local: block o of device c goes to device (c - o + 4) mod 8 of the same row. In each block of 128 slots the filled slots come first, 32 or more are filled, and every device fills one block completely. `intersection_entry_slot`: -1 marks an unused entry. A value q names slot q % 128 of block q // 128 that device (p + q // 128 - 8 // 2) mod 8 of the same row sends to this device p; every filled slot sent to a device is read by exactly one of its entries, unfilled ones by none; the first entry of every cell is used.
All inputs are finite; a program needn't handle non-finite values.
Results may differ from the reference program's by a relative error of at most 0.0015.
Values may be sent and summed in bfloat16 or wider, within the bound.
A program may use at most 64 MiB of HBM per device.

```python
import math
import jax
import jax.numpy as jnp
import numpy as np
from jax import lax

F = 8
NP = 16
MODES = 6
NFLUX = 4
NLAY = 20
K = 4
SUB = 2
SPAN = 8
E_DEV = 512
CAPE = 128
NROWS = 4
NCOLS = 8
SLOT_DEV = 1024
L_DEV = 256
ELEMS = 16384
LAND = 8192


def live_counts(key):
    key = jax.random.fold_in(key, 77)
    counts = jax.random.randint(key, (NROWS, NCOLS, SPAN), CAPE // K, CAPE + 1)
    row_ids = jnp.arange(NROWS, dtype=jnp.int32)[:, None, None]
    source_element_index = jnp.arange(NCOLS, dtype=jnp.int32)[None, :, None]
    block_ids = jnp.arange(SPAN, dtype=jnp.int32)[None, None, :]
    full_block = block_ids == (source_element_index + row_ids) % SPAN
    return jnp.where(full_block, CAPE, counts).astype(jnp.int32)


def draw_send_elem(key, part):
    counts = live_counts(key)
    key = jax.random.fold_in(key, 1)
    elements = jax.random.randint(key, (NROWS, NCOLS, SPAN, CAPE), 0, E_DEV)
    position = jnp.arange(CAPE, dtype=jnp.int32)
    table = jnp.where(position[None, None, None, :] < counts[..., None], elements, -1)
    return table.reshape(NROWS, NCOLS * SPAN, CAPE).astype(jnp.int32)


def draw_intersection_entry_slot(key, part):
    counts = live_counts(key)
    key = jax.random.fold_in(key, 2)
    key_slots, key_cells = jax.random.split(key)
    target_ids = jnp.arange(NCOLS, dtype=jnp.int32)[:, None]
    block_ids = jnp.arange(SPAN, dtype=jnp.int32)[None, :]
    sender_ids = ((target_ids + block_ids - SPAN // 2) % NCOLS).astype(jnp.int32)
    block_grid = jnp.broadcast_to(block_ids, (NCOLS, SPAN))
    received = counts[:, sender_ids, block_grid]
    position = jnp.arange(CAPE, dtype=jnp.int32)
    filled = position[None, None, None, :] < received[..., None]
    filled = filled.reshape(NROWS, NCOLS, SLOT_DEV)
    slot_ids = jnp.arange(SLOT_DEV, dtype=jnp.int32)
    noise = jax.random.randint(key_slots, (NROWS, NCOLS, SLOT_DEV), 0, 2 ** 17)
    score = jnp.where(filled, 0, 2 ** 29) + noise * SLOT_DEV + slot_ids[None, None, :]
    order = jnp.argsort(score, axis=-1, stable=True).astype(jnp.int32)
    ordered_fill = jnp.take_along_axis(filled, order, axis=-1)
    picked = jnp.where(ordered_fill, order, -1).astype(jnp.int32)
    grid = picked.reshape(NROWS, NCOLS, K, L_DEV)
    cell_ids = jnp.arange(L_DEV, dtype=jnp.int32)
    cell_noise = jax.random.randint(key_cells, (NROWS, NCOLS, L_DEV), 0, 2 ** 17) * L_DEV + cell_ids[None, None, :]
    cell_order = jnp.argsort(cell_noise, axis=-1, stable=True).astype(jnp.int32)
    grid = jnp.take_along_axis(grid, cell_order[:, :, None, :], axis=3)
    return jnp.transpose(grid, (2, 0, 1, 3)).reshape(K, NROWS * NCOLS * L_DEV).astype(jnp.int32)


def touch_ends(result, stream_key, least, high):
    shape = result.shape
    spot = [jax.random.randint(jax.random.fold_in(stream_key, axis), (), 0, shape[axis]) for axis in range(len(shape))]
    result = result.at[tuple(spot)].set(least)
    longest = shape.index(max(shape))
    spot[longest] = (spot[longest] + 1) % shape[longest]
    return result.at[tuple(spot)].set(high)


def block_scale(stream_key, shape, pieces, smallest, largest):
    def one(dim, shards_of):
        heights = jax.random.uniform(jax.random.fold_in(jax.random.fold_in(stream_key, 6), dim), (shards_of,), jnp.float32, smallest / len(pieces), largest / len(pieces))
        return jnp.repeat(jnp.exp(heights), shape[dim] // shards_of).reshape((-1,) + (1,) * (len(shape) - dim - 1))

    loudness = one(*pieces[0])
    for cut in pieces[1:]:
        loudness = loudness * one(*cut)
    return loudness


def bell_draw(key, extent, deviation, bound, cuts=(), held_as=jnp.bfloat16):
    result = jax.random.normal(key, extent, jnp.float32) * deviation
    if len(cuts) > 0:
        result = block_scale(key, extent, cuts, -0.22, 0.18) * result
    return jnp.clip(result, min=-bound, max=bound).astype(held_as)


def setup_inputs(seed: int = 0) -> dict:
    splits = jax.random.split(jax.random.key(seed), 14)
    return {
        "forcing": bell_draw(splits[0], (SUB, F, NP, ELEMS), 1.0, 6.0, ((3, 32),), jnp.float32),
        "elem_area": jnp.clip(jnp.exp(math.log(2.0) - 1.3862944 * jax.random.uniform(splits[1], (ELEMS,), jnp.float32) ** block_scale(splits[1], (ELEMS,), ((0, 32),), -0.2, 0.2)), 0.5, 2.0),
        "send_elem": draw_send_elem(jax.random.fold_in(splits[13], 71), 0),
        "intersection_entry_slot": draw_intersection_entry_slot(jax.random.fold_in(splits[13], 71), 0),
        "entry_weight": jnp.clip(jnp.exp(math.log(1.0) - 2.3025851 * jax.random.uniform(splits[4], (K, LAND), jnp.float32) ** block_scale(splits[4], (K, LAND), ((1, 32),), -0.2, 0.2)), 0.1, 1.0),
        "entry_coords": jnp.clip(jax.random.uniform(splits[5], (2, K, LAND), jnp.float32, -1.0, 1.0) * block_scale(splits[5], (2, K, LAND), ((2, 32),), -0.4, 0.0), -1.0, 1.0),
        "land_area": jnp.clip(jnp.exp(math.log(4.0) - 1.3862944 * jax.random.uniform(splits[6], (LAND,), jnp.float32) ** block_scale(splits[6], (LAND,), ((0, 32),), -0.2, 0.2)), 1.0, 4.0),
        "soil_temp": jnp.clip(0.5 + 1.0 * jax.random.uniform(splits[7], (NLAY, LAND), jnp.float32) ** block_scale(splits[7], (NLAY, LAND), ((1, 32),), -0.2, 0.2), 0.5, 1.5),
        "soil_cond": jnp.clip(jnp.exp(math.log(2.0) - 2.3025851 * jax.random.uniform(splits[8], (NLAY, LAND), jnp.float32) ** block_scale(splits[8], (NLAY, LAND), ((1, 32),), -0.2, 0.2)), 0.2, 2.0),
        "heat_cap": jnp.clip(jnp.exp(math.log(2.0) - 1.3862944 * jax.random.uniform(splits[9], (NLAY, LAND), jnp.float32) ** block_scale(splits[9], (NLAY, LAND), ((1, 32),), -0.2, 0.2)), 0.5, 2.0),
        "layer_count": touch_ends(jax.random.randint(splits[10], (LAND,), 8, NLAY + 1), jax.random.fold_in(splits[10], 1), 8, NLAY).astype(jnp.int32),
        "snow_count": touch_ends(jax.random.randint(splits[11], (LAND,), 0, 6), jax.random.fold_in(splits[11], 1), 0, 5).astype(jnp.int32),
        "mix": jnp.clip(jax.random.uniform(splits[12], (F,), jnp.float32, 0.3, 1.0), 0.3, 1.0),
    }


def legendre(degree, position):
    if degree == 0:
        return 1.0 + 0.0 * position
    if degree == 1:
        return position
    return 1.5 * position * position - 0.5

def modal_tables():
    lobatto_quadrature_points = np.array([-1.0, -1.0 / np.sqrt(5.0), 1.0 / np.sqrt(5.0), 1.0])
    gll_weights = np.array([1.0 / 6.0, 5.0 / 6.0, 5.0 / 6.0, 1.0 / 6.0])
    degree_pairs = [(0, 0), (1, 0), (0, 1), (2, 0), (1, 1), (0, 2)]
    projection_operator = np.zeros((6, 16))
    nodal_basis = np.zeros((16, 6))
    for first in range(4):
        for second in range(4):
            node = 4 * first + second
            for mode, pair in enumerate(degree_pairs):
                value = legendre(pair[0], lobatto_quadrature_points[first]) * legendre(pair[1], lobatto_quadrature_points[second])
                nodal_basis[node, mode] = value
                scale = (2 * pair[0] + 1) * (2 * pair[1] + 1) / 4.0
                projection_operator[mode, node] = gll_weights[first] * gll_weights[second] * scale * value
    return (jnp.asarray(projection_operator, dtype=jnp.float32), jnp.asarray(nodal_basis, dtype=jnp.float32))

def modal_basis(first_coord, second_coord):
    ones = jnp.ones_like(first_coord)
    return jnp.stack([ones, first_coord, second_coord, 1.5 * first_coord * first_coord - 0.5, first_coord * second_coord, 1.5 * second_coord * second_coord - 0.5])

def land_step(land_forcing, soil_state, soil_cond, heat_cap, layer_count, snow_count, mix):
    absorbed = 0.5 * lax.optimization_barrier(jnp.sum(mix[:, None] * land_forcing, axis=0))
    t_air = land_forcing[2]
    exchange_coef = 0.5 + 0.5 * land_forcing[4] * land_forcing[4]
    layer_index = lax.broadcasted_iota(jnp.int32, soil_state.shape, 0)
    active = layer_index < layer_count[None, :]
    in_snow = layer_index < snow_count[None, :]
    conduct = jnp.where(in_snow, 0.25 * soil_cond, soil_cond)
    linked = layer_index[1:] < layer_count[None, :]
    interface = jnp.where(linked, 2.0 * conduct[:-1] * conduct[1:] / (conduct[:-1] + conduct[1:]), 0.0)
    zero_row = jnp.zeros_like(soil_state[:1])
    upper_link = jnp.concatenate([zero_row, interface], axis=0)
    lower_link = jnp.concatenate([interface, zero_row], axis=0)
    surface = layer_index == 0
    diagonal = jnp.where(active, heat_cap + upper_link + lower_link + jnp.where(surface, exchange_coef[None, :], 0.0), 1.0)
    right_side = jnp.where(active, heat_cap * soil_state + jnp.where(surface, (absorbed + exchange_coef * t_air)[None, :], 0.0), soil_state)
    ratios = []
    shifted = []
    for depth_level in range(soil_state.shape[0]):
        lower_coef = -upper_link[depth_level]
        upper_coef = -lower_link[depth_level]
        if depth_level == 0:
            pivot = diagonal[0]
            shift = right_side[0] / pivot
        else:
            pivot = diagonal[depth_level] - lower_coef * ratios[-1]
            shift = (right_side[depth_level] - lower_coef * shifted[-1]) / pivot
        ratios.append(upper_coef / pivot)
        shifted.append(shift)
    solved = [shifted[-1]]
    for depth_level in reversed(range(soil_state.shape[0] - 1)):
        solved.insert(0, shifted[depth_level] - ratios[depth_level] * solved[0])
    solved = jnp.stack(solved)
    land_flux = jnp.stack([exchange_coef * (solved[0] - t_air), solved[0], interface[0] * (solved[0] - solved[1]), exchange_coef * land_forcing[3]])
    return (solved, land_flux)

def reference(forcing, elem_area, send_elem, intersection_entry_slot, entry_weight, entry_coords, land_area, soil_temp, soil_cond, heat_cap, layer_count, snow_count, mix):
    projection_operator, nodal_basis = modal_tables()
    modal_coefficients = jnp.einsum('polw,yl->pwoy', forcing, projection_operator, precision=lax.Precision.HIGHEST).astype(jnp.bfloat16)
    send_table = send_elem.reshape(NROWS, NCOLS, SPAN, CAPE)
    owner = jnp.arange(LAND, dtype=jnp.int32) // L_DEV
    owner_row = (owner // NCOLS)[None, :]
    owner_col = (owner % NCOLS)[None, :]
    live_entry = intersection_entry_slot >= 0
    entry_index = jnp.maximum(intersection_entry_slot, 0)
    source_block = entry_index // CAPE
    source_col = ((owner_col + source_block - SPAN // 2) % NCOLS).astype(jnp.int32)
    source_pos = entry_index % CAPE
    local_elem = send_table[owner_row, source_col, source_block, source_pos]
    source_element = ((owner_row * NCOLS + source_col) * E_DEV + jnp.maximum(local_elem, 0)).astype(jnp.int32)
    live_weight = jnp.where(live_entry, entry_weight, 0.0)
    entry_basis = modal_basis(entry_coords[0], entry_coords[1])
    total_weight = lax.optimization_barrier(jnp.sum(live_weight, axis=0))
    area_total = jnp.sum(elem_area)
    soil_state = soil_temp
    results = []
    for substep in range(SUB):
        intersection_entry_values = modal_coefficients[substep][source_element].astype(jnp.float32)
        at_points = jnp.einsum('klfm,mkl->fkl', intersection_entry_values, entry_basis, precision=lax.Precision.HIGHEST)
        land_forcing = lax.optimization_barrier(jnp.sum(live_weight[None] * at_points, axis=1)) / total_weight[None, :]
        soil_state, land_flux = land_step(land_forcing, soil_state, soil_cond, heat_cap, layer_count, snow_count, mix)
        contrib = live_weight[:, :, None, None] * jnp.transpose(land_flux)[None, :, :, None] * jnp.transpose(entry_basis, (1, 2, 0))[:, :, None, :]
        element_sum = jnp.zeros((ELEMS, NFLUX, MODES), jnp.float32).at[source_element.reshape(-1)].add(contrib.reshape(-1, NFLUX, MODES))
        element_coef = element_sum / elem_area[:, None, None]
        land_total = lax.optimization_barrier(jnp.sum(land_area[None, :] * land_flux, axis=1))
        atm_total = lax.optimization_barrier(jnp.sum(elem_area[:, None] * element_coef[:, :, 0], axis=0))
        correction = (land_total - atm_total) / area_total
        element_coef = element_coef.at[:, :, 0].add(correction[None, :])
        results.append(jnp.einsum('ejm,nm->jne', element_coef, nodal_basis, precision=lax.Precision.HIGHEST))
    return (jnp.stack(results), soil_state)
```

```python
import functools

import jax
import jax.numpy as jnp
import numpy as np
from jax import lax
from jax.experimental import pallas as pl
from jax.experimental.pallas import tpu as pltpu
from jax.sharding import PartitionSpec as P

MODES = 6
SUB = 2
FIELDS = 4
ROWS = SUB * FIELDS
NODES = 16
MESH = pl.DeviceIdType.MESH
F32 = jnp.float32
BF16 = jnp.bfloat16


def legendre(degree, position):
    if degree == 0:
        return 1.0 + 0.0 * position
    if degree == 1:
        return position
    return 1.5 * position * position - 0.5


def modal_tables():
    points = np.array([-1.0, -1.0 / np.sqrt(5.0), 1.0 / np.sqrt(5.0), 1.0])
    weights = np.array([1.0 / 6.0, 5.0 / 6.0, 5.0 / 6.0, 1.0 / 6.0])
    pairs = [(0, 0), (1, 0), (0, 1), (2, 0), (1, 1), (0, 2)]
    project = np.zeros((MODES, NODES))
    basis = np.zeros((NODES, MODES))
    for a in range(4):
        for b in range(4):
            for m, (i, j) in enumerate(pairs):
                value = legendre(i, points[a]) * legendre(j, points[b])
                basis[4 * a + b, m] = value
                scale = (2 * i + 1) * (2 * j + 1) / 4.0
                project[m, 4 * a + b] = weights[a] * weights[b] * scale * value
    return project, basis


def split_table(table):
    table = table.astype(np.float32)
    high = table.astype(BF16)
    low = (table - high.astype(np.float32)).astype(BF16)
    return jnp.asarray(np.concatenate([high, high, low], axis=1))


def block_tables():
    project, basis = modal_tables()
    wide_project = np.zeros((MODES * ROWS, ROWS * NODES))
    wide_basis = np.zeros((ROWS * NODES, MODES * ROWS))
    for m in range(MODES):
        for r in range(ROWS):
            wide_project[m * ROWS + r, r * NODES : (r + 1) * NODES] = project[m]
            wide_basis[r * NODES : (r + 1) * NODES, m * ROWS + r] = basis[:, m]
    return split_table(wide_project), split_table(wide_basis)


def split(values):
    high = values.astype(BF16)
    low = (values - high.astype(F32)).astype(BF16)
    return high, low


def dot(a, b):
    return jnp.dot(a, b, preferred_element_type=F32)


def dot_t(a, b):
    return lax.dot_general(a, b, (((1,), (1,)), ((), ())), preferred_element_type=F32)


def one_hot(mask):
    return jnp.where(mask, 1.0, 0.0).astype(BF16)


def weighted_basis(weight, u, v):
    return [
        weight,
        weight * u,
        weight * v,
        weight * (1.5 * u * u - 0.5),
        weight * (u * v),
        weight * (1.5 * v * v - 0.5),
    ]


def kernel(
    nrows,
    ncols,
    span,
    cap,
    stages,
    forcing_ref,
    area_ref,
    send_ref,
    slot_ref,
    weight_ref,
    coords_ref,
    land_area_ref,
    temp_ref,
    cond_ref,
    heat_ref,
    layers_ref,
    snow_ref,
    mix_ref,
    project_ref,
    basis_ref,
    out_ref,
    soil_ref,
    coef_send,
    coef_recv,
    point_send,
    point_recv,
    flux_send,
    flux_recv,
    total_send,
    total_recv,
    elem_hot,
    slot_hot,
    coef_sems,
    point_sems,
    flux_sems,
    total_sems,
):
    row, col = lax.axis_index("row"), lax.axis_index("col")
    half = span // 2
    elems = forcing_ref.shape[3]
    entries, cells = slot_ref.shape
    layers = temp_ref.shape[0]

    def device(dr, dc):
        return (lax.rem(row + dr % nrows, nrows), lax.rem(col + dc % ncols, ncols))

    offsets = {(0, d % ncols) for d in range(-half, half + 1)}
    for stage in stages:
        offsets |= set(stage)
    offsets = sorted(offsets - {(0, 0)})
    barrier = pltpu.get_barrier_semaphore()
    for dr, dc in offsets:
        pl.semaphore_signal(barrier, inc=1, device_id=device(dr, dc), device_id_type=MESH)

    rows = []
    for s in range(SUB):
        mixed = (0.5 * mix_ref[0]) * forcing_ref[s, 0]
        for f in range(1, forcing_ref.shape[1]):
            mixed = mixed + (0.5 * mix_ref[f]) * forcing_ref[s, f]
        rows += [mixed, forcing_ref[s, 2], forcing_ref[s, 3], forcing_ref[s, 4]]
    high, low = split(jnp.concatenate(rows, axis=0))
    coef = dot(project_ref[...], jnp.concatenate([high, low, high], axis=0)).astype(BF16)

    elem_iota = lax.broadcasted_iota(jnp.int32, (elems, cap), 0)
    for o in range(span):
        elem_hot[:, o * cap : (o + 1) * cap] = one_hot(elem_iota == send_ref[o : o + 1, :])
    sent = dot(coef, elem_hot[...]).astype(BF16)
    for o in range(span):
        coef_send[o] = sent[:, o * cap : (o + 1) * cap]

    pl.semaphore_wait(barrier, len(offsets))

    def exchange(source, target, sems, direction):
        copies = {}
        for o in range(span):
            if o == half:
                continue
            copies[o] = pltpu.make_async_remote_copy(
                src_ref=source.at[o],
                dst_ref=target.at[o],
                send_sem=sems.at[0, o],
                recv_sem=sems.at[1, o],
                device_id=device(0, direction * (half - o)),
                device_id_type=MESH,
            )
            copies[o].start()
        return copies

    coef_copies = exchange(coef_send, coef_recv, coef_sems, 1)

    q = slot_ref[...]
    weight = jnp.where(q >= 0, weight_ref[...], 0.0)
    weight_sum = jnp.sum(weight, axis=0, keepdims=True)
    share = weight / weight_sum

    def flat(values):
        return jnp.concatenate([values[k : k + 1, :] for k in range(entries)], axis=1)

    qf = flat(q)
    stacked = jnp.concatenate(
        [flat(coords_ref[0]), flat(coords_ref[1]), flat(weight), flat(share)], axis=0
    )
    stacked_high = stacked.astype(BF16).astype(F32)
    stacked = jnp.concatenate([stacked_high, stacked - stacked_high], axis=0)
    place_hot = one_hot(
        lax.broadcasted_iota(jnp.int32, (cap, entries * cells), 0) == (qf & (cap - 1))
    )
    by_block = jnp.concatenate(
        [
            jnp.where((qf >= o * cap) & (qf < (o + 1) * cap), stacked, 0.0)
            for o in range(span)
        ],
        axis=0,
    ).astype(BF16)
    points = dot_t(by_block, place_hot)
    for o in range(span):
        point_send[o] = points[o * 8 : (o + 1) * 8]
    point_copies = exchange(point_send, point_recv, point_sems, -1)

    place_iota = lax.broadcasted_iota(jnp.int32, (cap, cells), 0)
    for o in range(span):
        here = place_iota == q[0:1, :] - o * cap
        for k in range(1, entries):
            here = here | (place_iota == q[k : k + 1, :] - o * cap)
        slot_hot[o * cap : (o + 1) * cap, :] = one_hot(here)

    def lanes(blocks):
        return jnp.concatenate(blocks, axis=1)

    def slot_points(tiles):
        wide = lanes(tiles)
        wide = wide[0:4] + wide[4:8]
        return wide[0:1], wide[1:2], wide[2:3], wide[3:4]

    u, v, _, share_slot = slot_points([points[o * 8 : (o + 1) * 8] for o in range(span)])
    land_basis = weighted_basis(share_slot, u, v)

    layer_count, snow_count = layers_ref[...], snow_ref[...]
    heat = [heat_ref[z : z + 1, :] for z in range(layers)]
    start = [temp_ref[z : z + 1, :] for z in range(layers)]
    conduct = [
        jnp.where(z < snow_count, 0.25, 1.0) * cond_ref[z : z + 1, :] for z in range(layers)
    ]
    link = [
        jnp.where(
            z + 1 < layer_count,
            2.0 * conduct[z] * conduct[z + 1] / (conduct[z] + conduct[z + 1]),
            0.0,
        )
        for z in range(layers - 1)
    ]
    inverse, ratio, shift = [None] * layers, [None] * layers, [None] * layers
    for z in reversed(range(1, layers)):
        pivot = heat[z] + link[z - 1]
        right = heat[z] * start[z]
        if z + 1 < layers:
            pivot = pivot + link[z] * (1.0 - ratio[z + 1])
            right = right + link[z] * shift[z + 1]
        inverse[z] = 1.0 / pivot
        ratio[z] = link[z - 1] * inverse[z]
        shift[z] = right * inverse[z]
    base, gain = [jnp.zeros_like(heat[0])], [jnp.ones_like(heat[0])]
    for z in range(1, layers):
        base.append(shift[z] + ratio[z] * base[z - 1])
        gain.append(ratio[z] * gain[z - 1])
    shift_base, shift_gain = [None] * layers, [None] * layers
    for z in reversed(range(1, layers)):
        right_base, right_gain = heat[z] * base[z], heat[z] * gain[z]
        if z + 1 < layers:
            right_base = right_base + link[z] * shift_base[z + 1]
            right_gain = right_gain + link[z] * shift_gain[z + 1]
        shift_base[z] = right_base * inverse[z]
        shift_gain[z] = right_gain * inverse[z]
    top_pivot = heat[0] + link[0] * (1.0 - ratio[1])

    for o in coef_copies:
        coef_copies[o].wait_recv()
    got = [(coef_send if o == half else coef_recv)[o].astype(F32) for o in range(span)]
    at_points = jnp.zeros((ROWS, span * cap), F32)
    for m in range(MODES):
        at_points = at_points + land_basis[m] * lanes(
            [block[m * ROWS : (m + 1) * ROWS] for block in got]
        )
    high, low = split(at_points)
    gathered = dot(jnp.concatenate([high, low], axis=0), slot_hot[...])
    land = gathered[0:ROWS] + gathered[ROWS : 2 * ROWS]

    flux = []
    tops = []
    for s in range(SUB):
        absorbed, t_air, passed, driver = (
            land[s * FIELDS + i : s * FIELDS + i + 1] for i in range(FIELDS)
        )
        exch = 0.5 + 0.5 * driver * driver
        if s == 0:
            before, below = start[0], shift[1]
        else:
            before, below = tops[0], shift_base[1] + shift_gain[1] * tops[0]
        top = (heat[0] * before + absorbed + exch * t_air + link[0] * below) / (
            top_pivot + exch
        )
        second = below + ratio[1] * top
        tops.append(top)
        flux += [exch * (top - t_air), top, link[0] * (top - second), exch * passed]
    flux = jnp.concatenate(flux, axis=0)
    high, low = split(flux)
    spread = dot_t(jnp.concatenate([high, low], axis=0), slot_hot[...])
    spread = spread[0:ROWS] + spread[ROWS : 2 * ROWS]
    for o in range(span):
        flux_send[o] = spread[:, o * cap : (o + 1) * cap]
    flux_copies = exchange(flux_send, flux_recv, flux_sems, -1)

    excess = land_area_ref[...] - weight_sum
    partial = jnp.sum(excess * flux, axis=1, keepdims=True)
    lane = lax.broadcasted_iota(jnp.int32, (ROWS, cap), 1)
    place = lax.broadcasted_iota(jnp.int32, (ROWS, cap), 0)
    total = jnp.sum(jnp.where(lane == place, partial, 0.0), axis=0, keepdims=True)
    area = area_ref[...]
    area_total = jnp.sum(area, axis=1, keepdims=True)
    total = total + jnp.where(lane[0:1] == ROWS, area_total, 0.0)
    total_copies = []
    first = 0

    def send_total(stage, first, total):
        total_send[first] = total
        copies = []
        for i, (dr, dc) in enumerate(stage):
            copy = pltpu.make_async_remote_copy(
                src_ref=total_send.at[first],
                dst_ref=total_recv.at[first + i],
                send_sem=total_sems.at[0, first + i],
                recv_sem=total_sems.at[1, first + i],
                device_id=device(dr, dc),
                device_id_type=MESH,
            )
            copy.start()
            copies.append(copy)
        return copies

    def sum_total(stage, first, total, copies):
        for copy in copies:
            copy.wait_recv()
        for i in range(len(stage)):
            total = total + total_recv[first + i]
        return total

    pending = send_total(stages[0], 0, total)
    total_copies += pending

    rest, slope = jnp.zeros_like(heat[0]), jnp.zeros_like(heat[0])
    soil_ref[0:1, :] = tops[1]
    for z in range(1, layers):
        rest = shift_base[z] + ratio[z] * rest
        slope = shift_gain[z] + ratio[z] * slope
        soil_ref[z : z + 1, :] = rest + slope * tops[0] + gain[z] * tops[1]

    for o in point_copies:
        point_copies[o].wait_recv()
    u, v, weight_slot, _ = slot_points(
        [(point_send if o == half else point_recv)[o] for o in range(span)]
    )
    elem_basis = weighted_basis(weight_slot, u, v)
    for o in flux_copies:
        flux_copies[o].wait_recv()
    back = lanes([(flux_send if o == half else flux_recv)[o] for o in range(span)])
    terms = jnp.concatenate([elem_basis[m] * back for m in range(MODES)], axis=0)
    high, low = split(terms)
    summed = dot_t(jnp.concatenate([high, low], axis=0), elem_hot[...])
    count = MODES * ROWS
    element_coef = (summed[0:count] + summed[count : 2 * count]) / area
    high, low = split(element_coef)
    nodes = dot(basis_ref[...], jnp.concatenate([high, low, high], axis=0))

    total = sum_total(stages[0], 0, total, pending)
    first = len(stages[0])
    for stage in stages[1:]:
        pending = send_total(stage, first, total)
        total_copies += pending
        total = sum_total(stage, first, total, pending)
        first += len(stage)
    spread_total = jnp.broadcast_to(total, (ROWS, cap))
    budget = jnp.sum(jnp.where(lane == place, spread_total, 0.0), axis=1, keepdims=True)
    all_area = jnp.sum(jnp.where(lane == ROWS, spread_total, 0.0), axis=1, keepdims=True)
    correction = budget / all_area
    for r in range(ROWS):
        out_ref[r // FIELDS, r % FIELDS] = (
            nodes[r * NODES : (r + 1) * NODES] + correction[r : r + 1, :]
        )

    for copies in (coef_copies, point_copies, flux_copies):
        for o in copies:
            copies[o].wait_send()
    for copy in total_copies:
        copy.wait_send()


def local(nrows, ncols, *args):
    (
        forcing,
        elem_area,
        send_elem,
        slots,
        entry_weight,
        entry_coords,
        land_area,
        soil_temp,
        soil_cond,
        heat_cap,
        layer_count,
        snow_count,
        mix,
    ) = args
    _, span, cap = send_elem.shape
    elems = forcing.shape[3]
    cells = land_area.shape[0]
    if nrows * ncols <= 64:
        stages = [
            [(r, c) for r in range(nrows) for c in range(ncols) if (r, c) != (0, 0)]
        ]
    else:
        stages = [[(r, 0) for r in range(1, nrows)], [(0, c) for c in range(1, ncols)]]
    peers = sum(len(stage) for stage in stages)
    project, basis = block_tables()
    vmem = pl.BlockSpec(memory_space=pltpu.VMEM)
    smem = pl.BlockSpec(memory_space=pltpu.SMEM)
    return pl.pallas_call(
        functools.partial(kernel, nrows, ncols, span, cap, stages),
        out_shape=(
            jax.ShapeDtypeStruct((SUB, FIELDS, NODES, elems), F32),
            jax.ShapeDtypeStruct(soil_temp.shape, F32),
        ),
        in_specs=[vmem] * 12 + [smem] + [vmem] * 2,
        out_specs=(vmem, vmem),
        scratch_shapes=[
            pltpu.VMEM((span, MODES * ROWS, cap), BF16),
            pltpu.VMEM((span, MODES * ROWS, cap), BF16),
            pltpu.VMEM((span, 8, cap), F32),
            pltpu.VMEM((span, 8, cap), F32),
            pltpu.VMEM((span, ROWS, cap), F32),
            pltpu.VMEM((span, ROWS, cap), F32),
            pltpu.VMEM((peers, 1, cap), F32),
            pltpu.VMEM((peers, 1, cap), F32),
            pltpu.VMEM((elems, span * cap), BF16),
            pltpu.VMEM((span * cap, cells), BF16),
            pltpu.SemaphoreType.DMA((2, span)),
            pltpu.SemaphoreType.DMA((2, span)),
            pltpu.SemaphoreType.DMA((2, span)),
            pltpu.SemaphoreType.DMA((2, peers)),
        ],
        compiler_params=pltpu.CompilerParams(
            collective_id=0, has_side_effects=True, vmem_limit_bytes=32 * 1024 * 1024
        ),
    )(
        forcing,
        elem_area.reshape(1, elems),
        send_elem.reshape(span, cap),
        slots,
        entry_weight,
        entry_coords,
        land_area.reshape(1, cells),
        soil_temp,
        soil_cond,
        heat_cap,
        layer_count.reshape(1, cells),
        snow_count.reshape(1, cells),
        mix,
        project,
        basis,
    )


def solution(mesh):
    placed = (
        P(None, None, None, ("row", "col")),
        P(("row", "col")),
        P("row", "col", None),
        P(None, ("row", "col")),
        P(None, ("row", "col")),
        P(None, None, ("row", "col")),
        P(("row", "col")),
        P(None, ("row", "col")),
        P(None, ("row", "col")),
        P(None, ("row", "col")),
        P(("row", "col")),
        P(("row", "col")),
        P(),
    )
    return jax.shard_map(
        functools.partial(local, mesh.shape["row"], mesh.shape["col"]),
        mesh=mesh,
        in_specs=placed,
        out_specs=(P(None, None, None, ("row", "col")), P(None, ("row", "col"))),
        check_vma=False,
    )
```

```python
import functools

import jax
import jax.numpy as jnp
import numpy as np
from jax import lax
from jax.experimental import pallas as pl
from jax.experimental.pallas import tpu as pltpu
from jax.sharding import PartitionSpec as P

MODES = 6
SUB = 2
FIELDS = 4
ROWS = SUB * FIELDS
NODES = 16
LOAD_ORDER = (0, 12, 13, 2, 3, 4, 5, 7, 8, 9, 10, 11, 1, 6, 14)
MESH = pl.DeviceIdType.MESH
F32 = jnp.float32
BF16 = jnp.bfloat16


def legendre(degree, position):
    if degree == 0:
        return 1.0 + 0.0 * position
    if degree == 1:
        return position
    return 1.5 * position * position - 0.5


def modal_tables():
    points = np.array([-1.0, -1.0 / np.sqrt(5.0), 1.0 / np.sqrt(5.0), 1.0])
    weights = np.array([1.0 / 6.0, 5.0 / 6.0, 5.0 / 6.0, 1.0 / 6.0])
    pairs = [(0, 0), (1, 0), (0, 1), (2, 0), (1, 1), (0, 2)]
    project = np.zeros((MODES, NODES))
    basis = np.zeros((NODES, MODES))
    for a in range(4):
        for b in range(4):
            for m, (i, j) in enumerate(pairs):
                value = legendre(i, points[a]) * legendre(j, points[b])
                basis[4 * a + b, m] = value
                scale = (2 * i + 1) * (2 * j + 1) / 4.0
                project[m, 4 * a + b] = weights[a] * weights[b] * scale * value
    return project, basis


def split_table(table):
    table = table.astype(np.float32)
    high = table.astype(BF16)
    low = (table - high.astype(np.float32)).astype(BF16)
    return jnp.asarray(np.concatenate([high, high, low], axis=1).astype(np.float32))


def block_tables():
    project, basis = modal_tables()
    wide_project = np.zeros((MODES * ROWS, ROWS * NODES))
    wide_basis = np.zeros((ROWS * NODES, MODES * ROWS))
    for m in range(MODES):
        for r in range(ROWS):
            wide_project[m * ROWS + r, r * NODES : (r + 1) * NODES] = project[m]
            wide_basis[r * NODES : (r + 1) * NODES, m * ROWS + r] = basis[:, m]
    return split_table(wide_project), split_table(wide_basis)


def split(values):
    high = values.astype(BF16)
    low = (values - high.astype(F32)).astype(BF16)
    return high, low


def dot(a, b):
    return jnp.dot(a, b, preferred_element_type=F32)


def dot_t(a, b):
    return lax.dot_general(a, b, (((1,), (1,)), ((), ())), preferred_element_type=F32)


def one_hot(mask):
    return jnp.where(mask, 1.0, 0.0).astype(BF16)


def weighted_basis(weight, u, v):
    return [
        weight,
        weight * u,
        weight * v,
        weight * (1.5 * u * u - 0.5),
        weight * (u * v),
        weight * (1.5 * v * v - 0.5),
    ]


def kernel(
    nrows,
    ncols,
    span,
    cap,
    stages,
    *refs,
):
    operands, (out_ref, soil_ref), refs = refs[:15], refs[15:17], refs[17:]
    held, refs = refs[:15], refs[15:]
    (
    coef_send,
    coef_recv,
    point_send,
    point_recv,
    flux_send,
    flux_recv,
    total_send,
    total_recv,
    elem_hot,
    slot_hot,
    coef_sems,
    point_sems,
    flux_sems,
    total_sems,
        load_sems,
    ) = refs
    (
        forcing_ref,
        area_ref,
        send_ref,
        slot_ref,
        weight_ref,
        coords_ref,
        land_area_ref,
        temp_ref,
        cond_ref,
        heat_ref,
        layers_ref,
        snow_ref,
        mix_ref,
        project_ref,
        basis_ref,
    ) = held
    loads = [
        pltpu.make_async_copy(operands[i], held[i], load_sems.at[i]) for i in range(15)
    ]
    for i in LOAD_ORDER:
        loads[i].start()
    row, col = lax.axis_index("row"), lax.axis_index("col")
    half = span // 2
    elems = forcing_ref.shape[3]
    entries, cells = slot_ref.shape
    layers = temp_ref.shape[0]

    def device(dr, dc):
        return (lax.rem(row + dr % nrows, nrows), lax.rem(col + dc % ncols, ncols))

    offsets = {(0, d % ncols) for d in range(-half, half + 1)}
    for stage in stages:
        offsets |= set(stage)
    offsets = sorted(offsets - {(0, 0)})
    barrier = pltpu.get_barrier_semaphore()
    for dr, dc in offsets:
        pl.semaphore_signal(barrier, inc=1, device_id=device(dr, dc), device_id_type=MESH)

    for i in (0, 12, 13, 2):
        loads[i].wait()

    rows = []
    for s in range(SUB):
        mixed = (0.5 * mix_ref[0]) * forcing_ref[s, 0]
        for f in range(1, forcing_ref.shape[1]):
            mixed = mixed + (0.5 * mix_ref[f]) * forcing_ref[s, f]
        rows += [mixed, forcing_ref[s, 2], forcing_ref[s, 3], forcing_ref[s, 4]]
    high, low = split(jnp.concatenate(rows, axis=0))
    coef = dot(project_ref[...].astype(BF16), jnp.concatenate([high, low, high], axis=0)).astype(BF16)

    elem_iota = lax.broadcasted_iota(jnp.int32, (elems, cap), 0)
    for o in range(span):
        elem_hot[:, o * cap : (o + 1) * cap] = one_hot(elem_iota == send_ref[o : o + 1, :])
    sent = dot(coef, elem_hot[...]).astype(BF16)
    for o in range(span):
        coef_send[o] = sent[:, o * cap : (o + 1) * cap]

    pl.semaphore_wait(barrier, len(offsets))

    def exchange(source, target, sems, direction):
        copies = {}
        for o in range(span):
            if o == half:
                continue
            copies[o] = pltpu.make_async_remote_copy(
                src_ref=source.at[o],
                dst_ref=target.at[o],
                send_sem=sems.at[0, o],
                recv_sem=sems.at[1, o],
                device_id=device(0, direction * (half - o)),
                device_id_type=MESH,
            )
            copies[o].start()
        return copies

    coef_copies = exchange(coef_send, coef_recv, coef_sems, 1)

    for i in (3, 4, 5):
        loads[i].wait()

    q = slot_ref[...]
    weight = jnp.where(q >= 0, weight_ref[...], 0.0)
    weight_sum = jnp.sum(weight, axis=0, keepdims=True)
    share = weight / weight_sum

    def flat(values):
        return jnp.concatenate([values[k : k + 1, :] for k in range(entries)], axis=1)

    qf = flat(q)
    stacked = jnp.concatenate(
        [flat(coords_ref[0]), flat(coords_ref[1]), flat(weight), flat(share)], axis=0
    )
    stacked_high = stacked.astype(BF16).astype(F32)
    stacked = jnp.concatenate([stacked_high, stacked - stacked_high], axis=0)
    place_hot = one_hot(
        lax.broadcasted_iota(jnp.int32, (cap, entries * cells), 0) == (qf & (cap - 1))
    )
    by_block = jnp.concatenate(
        [
            jnp.where((qf >= o * cap) & (qf < (o + 1) * cap), stacked, 0.0)
            for o in range(span)
        ],
        axis=0,
    ).astype(BF16)
    points = dot_t(by_block, place_hot)
    for o in range(span):
        point_send[o] = points[o * 8 : (o + 1) * 8]
    point_copies = exchange(point_send, point_recv, point_sems, -1)

    place_iota = lax.broadcasted_iota(jnp.int32, (cap, cells), 0)
    for o in range(span):
        here = place_iota == q[0:1, :] - o * cap
        for k in range(1, entries):
            here = here | (place_iota == q[k : k + 1, :] - o * cap)
        slot_hot[o * cap : (o + 1) * cap, :] = one_hot(here)

    def lanes(blocks):
        return jnp.concatenate(blocks, axis=1)

    def slot_points(tiles):
        wide = lanes(tiles)
        wide = wide[0:4] + wide[4:8]
        return wide[0:1], wide[1:2], wide[2:3], wide[3:4]

    u, v, _, share_slot = slot_points([points[o * 8 : (o + 1) * 8] for o in range(span)])
    land_basis = weighted_basis(share_slot, u, v)

    for i in (7, 8, 9, 10, 11, 1, 6, 14):
        loads[i].wait()
    layer_count, snow_count = layers_ref[...], snow_ref[...]
    heat = [heat_ref[z : z + 1, :] for z in range(layers)]
    start = [temp_ref[z : z + 1, :] for z in range(layers)]
    conduct = [
        jnp.where(z < snow_count, 0.25, 1.0) * cond_ref[z : z + 1, :] for z in range(layers)
    ]
    link = [
        jnp.where(
            z + 1 < layer_count,
            2.0 * conduct[z] * conduct[z + 1] / (conduct[z] + conduct[z + 1]),
            0.0,
        )
        for z in range(layers - 1)
    ]
    inverse, ratio, shift = [None] * layers, [None] * layers, [None] * layers
    for z in reversed(range(1, layers)):
        pivot = heat[z] + link[z - 1]
        right = heat[z] * start[z]
        if z + 1 < layers:
            pivot = pivot + link[z] * (1.0 - ratio[z + 1])
            right = right + link[z] * shift[z + 1]
        inverse[z] = 1.0 / pivot
        ratio[z] = link[z - 1] * inverse[z]
        shift[z] = right * inverse[z]
    base, gain = [jnp.zeros_like(heat[0])], [jnp.ones_like(heat[0])]
    for z in range(1, layers):
        base.append(shift[z] + ratio[z] * base[z - 1])
        gain.append(ratio[z] * gain[z - 1])
    shift_base, shift_gain = [None] * layers, [None] * layers
    for z in reversed(range(1, layers)):
        right_base, right_gain = heat[z] * base[z], heat[z] * gain[z]
        if z + 1 < layers:
            right_base = right_base + link[z] * shift_base[z + 1]
            right_gain = right_gain + link[z] * shift_gain[z + 1]
        shift_base[z] = right_base * inverse[z]
        shift_gain[z] = right_gain * inverse[z]
    top_pivot = heat[0] + link[0] * (1.0 - ratio[1])

    for o in coef_copies:
        coef_copies[o].wait_recv()
    got = [(coef_send if o == half else coef_recv)[o].astype(F32) for o in range(span)]
    at_points = jnp.zeros((ROWS, span * cap), F32)
    for m in range(MODES):
        at_points = at_points + land_basis[m] * lanes(
            [block[m * ROWS : (m + 1) * ROWS] for block in got]
        )
    high, low = split(at_points)
    gathered = dot(jnp.concatenate([high, low], axis=0), slot_hot[...])
    land = gathered[0:ROWS] + gathered[ROWS : 2 * ROWS]

    flux = []
    tops = []
    for s in range(SUB):
        absorbed, t_air, passed, driver = (
            land[s * FIELDS + i : s * FIELDS + i + 1] for i in range(FIELDS)
        )
        exch = 0.5 + 0.5 * driver * driver
        if s == 0:
            before, below = start[0], shift[1]
        else:
            before, below = tops[0], shift_base[1] + shift_gain[1] * tops[0]
        top = (heat[0] * before + absorbed + exch * t_air + link[0] * below) / (
            top_pivot + exch
        )
        second = below + ratio[1] * top
        tops.append(top)
        flux += [exch * (top - t_air), top, link[0] * (top - second), exch * passed]
    flux = jnp.concatenate(flux, axis=0)
    high, low = split(flux)
    spread = dot_t(jnp.concatenate([high, low], axis=0), slot_hot[...])
    spread = spread[0:ROWS] + spread[ROWS : 2 * ROWS]
    for o in range(span):
        flux_send[o] = spread[:, o * cap : (o + 1) * cap]
    flux_copies = exchange(flux_send, flux_recv, flux_sems, -1)

    excess = land_area_ref[...] - weight_sum
    partial = jnp.sum(excess * flux, axis=1, keepdims=True)
    lane = lax.broadcasted_iota(jnp.int32, (ROWS, cap), 1)
    place = lax.broadcasted_iota(jnp.int32, (ROWS, cap), 0)
    total = jnp.sum(jnp.where(lane == place, partial, 0.0), axis=0, keepdims=True)
    area = area_ref[...]
    area_total = jnp.sum(area, axis=1, keepdims=True)
    total = total + jnp.where(lane[0:1] == ROWS, area_total, 0.0)
    total_copies = []
    first = 0

    def send_total(stage, first, total):
        total_send[first] = total
        copies = []
        for i, (dr, dc) in enumerate(stage):
            copy = pltpu.make_async_remote_copy(
                src_ref=total_send.at[first],
                dst_ref=total_recv.at[first + i],
                send_sem=total_sems.at[0, first + i],
                recv_sem=total_sems.at[1, first + i],
                device_id=device(dr, dc),
                device_id_type=MESH,
            )
            copy.start()
            copies.append(copy)
        return copies

    def sum_total(stage, first, total, copies):
        for copy in copies:
            copy.wait_recv()
        for i in range(len(stage)):
            total = total + total_recv[first + i]
        return total

    pending = send_total(stages[0], 0, total)
    total_copies += pending

    rest, slope = jnp.zeros_like(heat[0]), jnp.zeros_like(heat[0])
    soil_ref[0:1, :] = tops[1]
    for z in range(1, layers):
        rest = shift_base[z] + ratio[z] * rest
        slope = shift_gain[z] + ratio[z] * slope
        soil_ref[z : z + 1, :] = rest + slope * tops[0] + gain[z] * tops[1]

    for o in point_copies:
        point_copies[o].wait_recv()
    u, v, weight_slot, _ = slot_points(
        [(point_send if o == half else point_recv)[o] for o in range(span)]
    )
    elem_basis = weighted_basis(weight_slot, u, v)
    for o in flux_copies:
        flux_copies[o].wait_recv()
    back = lanes([(flux_send if o == half else flux_recv)[o] for o in range(span)])
    terms = jnp.concatenate([elem_basis[m] * back for m in range(MODES)], axis=0)
    high, low = split(terms)
    summed = dot_t(jnp.concatenate([high, low], axis=0), elem_hot[...])
    count = MODES * ROWS
    element_coef = (summed[0:count] + summed[count : 2 * count]) / area
    high, low = split(element_coef)
    nodes = dot(basis_ref[...].astype(BF16), jnp.concatenate([high, low, high], axis=0))

    total = sum_total(stages[0], 0, total, pending)
    first = len(stages[0])
    for stage in stages[1:]:
        pending = send_total(stage, first, total)
        total_copies += pending
        total = sum_total(stage, first, total, pending)
        first += len(stage)
    spread_total = jnp.broadcast_to(total, (ROWS, cap))
    budget = jnp.sum(jnp.where(lane == place, spread_total, 0.0), axis=1, keepdims=True)
    all_area = jnp.sum(jnp.where(lane == ROWS, spread_total, 0.0), axis=1, keepdims=True)
    correction = budget / all_area
    for r in range(ROWS):
        out_ref[r // FIELDS, r % FIELDS] = (
            nodes[r * NODES : (r + 1) * NODES] + correction[r : r + 1, :]
        )

    for copies in (coef_copies, point_copies, flux_copies):
        for o in copies:
            copies[o].wait_send()
    for copy in total_copies:
        copy.wait_send()


def local(nrows, ncols, *args):
    (
        forcing,
        elem_area,
        send_elem,
        slots,
        entry_weight,
        entry_coords,
        land_area,
        soil_temp,
        soil_cond,
        heat_cap,
        layer_count,
        snow_count,
        mix,
    ) = args
    _, span, cap = send_elem.shape
    elems = forcing.shape[3]
    cells = land_area.shape[0]
    if nrows * ncols <= 64:
        stages = [
            [(r, c) for r in range(nrows) for c in range(ncols) if (r, c) != (0, 0)]
        ]
    else:
        stages = [[(r, 0) for r in range(1, nrows)], [(0, c) for c in range(1, ncols)]]
    peers = sum(len(stage) for stage in stages)
    project, basis = block_tables()
    vmem = pl.BlockSpec(memory_space=pltpu.VMEM)
    hbm = pl.BlockSpec(memory_space=pltpu.HBM)
    operands = (
        forcing,
        elem_area.reshape(1, elems),
        send_elem.reshape(span, cap),
        slots,
        entry_weight,
        entry_coords,
        land_area.reshape(1, cells),
        soil_temp,
        soil_cond,
        heat_cap,
        layer_count.reshape(1, cells),
        snow_count.reshape(1, cells),
        mix,
        project,
        basis,
    )
    held = [
        (pltpu.SMEM if i == 12 else pltpu.VMEM)(x.shape, x.dtype)
        for i, x in enumerate(operands)
    ]
    return pl.pallas_call(
        functools.partial(kernel, nrows, ncols, span, cap, stages),
        out_shape=(
            jax.ShapeDtypeStruct((SUB, FIELDS, NODES, elems), F32),
            jax.ShapeDtypeStruct(soil_temp.shape, F32),
        ),
        in_specs=[hbm] * 15,
        out_specs=(vmem, vmem),
        scratch_shapes=held
        + [
            pltpu.VMEM((span, MODES * ROWS, cap), BF16),
            pltpu.VMEM((span, MODES * ROWS, cap), BF16),
            pltpu.VMEM((span, 8, cap), F32),
            pltpu.VMEM((span, 8, cap), F32),
            pltpu.VMEM((span, ROWS, cap), F32),
            pltpu.VMEM((span, ROWS, cap), F32),
            pltpu.VMEM((peers, 1, cap), F32),
            pltpu.VMEM((peers, 1, cap), F32),
            pltpu.VMEM((elems, span * cap), BF16),
            pltpu.VMEM((span * cap, cells), BF16),
            pltpu.SemaphoreType.DMA((2, span)),
            pltpu.SemaphoreType.DMA((2, span)),
            pltpu.SemaphoreType.DMA((2, span)),
            pltpu.SemaphoreType.DMA((2, peers)),
            pltpu.SemaphoreType.DMA((15,)),
        ],
        compiler_params=pltpu.CompilerParams(
            collective_id=0, has_side_effects=True, vmem_limit_bytes=60 * 1024 * 1024
        ),
    )(*operands)


def solution(mesh):
    placed = (
        P(None, None, None, ("row", "col")),
        P(("row", "col")),
        P("row", "col", None),
        P(None, ("row", "col")),
        P(None, ("row", "col")),
        P(None, None, ("row", "col")),
        P(("row", "col")),
        P(None, ("row", "col")),
        P(None, ("row", "col")),
        P(None, ("row", "col")),
        P(("row", "col")),
        P(("row", "col")),
        P(),
    )
    return jax.shard_map(
        functools.partial(local, mesh.shape["row"], mesh.shape["col"]),
        mesh=mesh,
        in_specs=placed,
        out_specs=(P(None, None, None, ("row", "col")), P(None, ("row", "col"))),
        check_vma=False,
    )
```

```python
import functools

import jax
import jax.numpy as jnp
import numpy as np
from jax import lax
from jax.experimental import pallas as pl
from jax.experimental.pallas import tpu as pltpu
from jax.sharding import PartitionSpec as P

MODES = 6
SUB = 2
FIELDS = 4
ROWS = SUB * FIELDS
NODES = 16
LOAD_ORDER = (0, 12, 13, 2, 3, 4, 5, 7, 8, 9, 10, 11, 1, 6, 14)
MESH = pl.DeviceIdType.MESH
F32 = jnp.float32
BF16 = jnp.bfloat16


def legendre(degree, position):
    if degree == 0:
        return 1.0 + 0.0 * position
    if degree == 1:
        return position
    return 1.5 * position * position - 0.5


def modal_tables():
    points = np.array([-1.0, -1.0 / np.sqrt(5.0), 1.0 / np.sqrt(5.0), 1.0])
    weights = np.array([1.0 / 6.0, 5.0 / 6.0, 5.0 / 6.0, 1.0 / 6.0])
    pairs = [(0, 0), (1, 0), (0, 1), (2, 0), (1, 1), (0, 2)]
    project = np.zeros((MODES, NODES))
    basis = np.zeros((NODES, MODES))
    for a in range(4):
        for b in range(4):
            for m, (i, j) in enumerate(pairs):
                value = legendre(i, points[a]) * legendre(j, points[b])
                basis[4 * a + b, m] = value
                scale = (2 * i + 1) * (2 * j + 1) / 4.0
                project[m, 4 * a + b] = weights[a] * weights[b] * scale * value
    return project, basis


def split_table(table):
    table = table.astype(np.float32)
    high = table.astype(BF16)
    low = (table - high.astype(np.float32)).astype(BF16)
    return jnp.asarray(np.concatenate([high, high, low], axis=1).astype(np.float32))


def block_tables():
    project, basis = modal_tables()
    wide_project = np.zeros((MODES * ROWS, ROWS * NODES))
    wide_basis = np.zeros((ROWS * NODES, MODES * ROWS))
    for m in range(MODES):
        for r in range(ROWS):
            wide_project[m * ROWS + r, r * NODES : (r + 1) * NODES] = project[m]
            wide_basis[r * NODES : (r + 1) * NODES, m * ROWS + r] = basis[:, m]
    return split_table(wide_project), split_table(wide_basis)


def split(values):
    high = values.astype(BF16)
    low = (values - high.astype(F32)).astype(BF16)
    return high, low


def dot(a, b):
    return jnp.dot(a, b, preferred_element_type=F32)


def dot_t(a, b):
    return lax.dot_general(a, b, (((1,), (1,)), ((), ())), preferred_element_type=F32)


def one_hot(mask):
    return jnp.where(mask, 1.0, 0.0).astype(BF16)


def weighted_basis(weight, u, v):
    return [
        weight,
        weight * u,
        weight * v,
        weight * (1.5 * u * u - 0.5),
        weight * (u * v),
        weight * (1.5 * v * v - 0.5),
    ]


def kernel(
    nrows,
    ncols,
    span,
    cap,
    stages,
    *refs,
):
    operands, (out_ref, soil_ref), refs = refs[:15], refs[15:17], refs[17:]
    held, refs = refs[:15], refs[15:]
    (
    coef_send,
    coef_recv,
    point_send,
    point_recv,
    flux_send,
    flux_recv,
    total_send,
    total_recv,
    elem_hot,
    slot_hot,
    coef_sems,
    point_sems,
    flux_sems,
    total_sems,
        load_sems,
    ) = refs
    (
        forcing_ref,
        area_ref,
        send_ref,
        slot_ref,
        weight_ref,
        coords_ref,
        land_area_ref,
        temp_ref,
        cond_ref,
        heat_ref,
        layers_ref,
        snow_ref,
        mix_ref,
        project_ref,
        basis_ref,
    ) = held
    loads = [
        pltpu.make_async_copy(operands[i], held[i], load_sems.at[i]) for i in range(15)
    ]
    for i in LOAD_ORDER:
        loads[i].start()
    row, col = lax.axis_index("row"), lax.axis_index("col")
    half = span // 2
    elems = forcing_ref.shape[3]
    entries, cells = slot_ref.shape
    layers = temp_ref.shape[0]

    def device(dr, dc):
        return (lax.rem(row + dr % nrows, nrows), lax.rem(col + dc % ncols, ncols))

    offsets = {(0, d % ncols) for d in range(-half, half + 1)}
    for stage in stages:
        offsets |= set(stage)
    offsets = sorted(offsets - {(0, 0)})
    barrier = pltpu.get_barrier_semaphore()
    for dr, dc in offsets:
        pl.semaphore_signal(barrier, inc=1, device_id=device(dr, dc), device_id_type=MESH)

    for i in (0, 12, 13, 2):
        loads[i].wait()

    rows = []
    for s in range(SUB):
        mixed = (0.5 * mix_ref[0]) * forcing_ref[s, 0]
        for f in range(1, forcing_ref.shape[1]):
            mixed = mixed + (0.5 * mix_ref[f]) * forcing_ref[s, f]
        rows += [mixed, forcing_ref[s, 2], forcing_ref[s, 3], forcing_ref[s, 4]]
    high, low = split(jnp.concatenate(rows, axis=0))
    coef = dot(project_ref[...].astype(BF16), jnp.concatenate([high, low, high], axis=0)).astype(BF16)

    elem_iota = lax.broadcasted_iota(jnp.int32, (elems, cap), 0)
    for o in range(span):
        elem_hot[:, o * cap : (o + 1) * cap] = one_hot(elem_iota == send_ref[o : o + 1, :])
    sent = dot(coef, elem_hot[...]).astype(BF16)
    for o in range(span):
        coef_send[o] = sent[:, o * cap : (o + 1) * cap]

    pl.semaphore_wait(barrier, len(offsets))

    def exchange(source, target, sems, direction):
        copies = {}
        for o in range(span):
            if o == half:
                continue
            copies[o] = pltpu.make_async_remote_copy(
                src_ref=source.at[o],
                dst_ref=target.at[o],
                send_sem=sems.at[0, o],
                recv_sem=sems.at[1, o],
                device_id=device(0, direction * (half - o)),
                device_id_type=MESH,
            )
            copies[o].start()
        return copies

    coef_copies = exchange(coef_send, coef_recv, coef_sems, 1)

    for i in (3, 4, 5):
        loads[i].wait()

    q = slot_ref[...]
    weight = jnp.where(q >= 0, weight_ref[...], 0.0)
    weight_sum = jnp.sum(weight, axis=0, keepdims=True)
    share = weight / weight_sum

    def flat(values):
        return jnp.concatenate([values[k : k + 1, :] for k in range(entries)], axis=1)

    qf = flat(q)
    stacked = jnp.concatenate(
        [flat(coords_ref[0]), flat(coords_ref[1]), flat(weight), flat(share)], axis=0
    )
    stacked_high = stacked.astype(BF16).astype(F32)
    stacked = jnp.concatenate([stacked_high, stacked - stacked_high], axis=0)
    place_hot = one_hot(
        lax.broadcasted_iota(jnp.int32, (cap, entries * cells), 0) == (qf & (cap - 1))
    )
    by_block = jnp.concatenate(
        [
            jnp.where((qf >= o * cap) & (qf < (o + 1) * cap), stacked, 0.0)
            for o in range(span)
        ],
        axis=0,
    ).astype(BF16)
    points = dot_t(by_block, place_hot)
    for o in range(span):
        point_send[o] = points[o * 8 : (o + 1) * 8]
    point_copies = exchange(point_send, point_recv, point_sems, -1)

    place_iota = lax.broadcasted_iota(jnp.int32, (cap, cells), 0)
    for o in range(span):
        here = place_iota == q[0:1, :] - o * cap
        for k in range(1, entries):
            here = here | (place_iota == q[k : k + 1, :] - o * cap)
        slot_hot[o * cap : (o + 1) * cap, :] = one_hot(here)

    def lanes(blocks):
        return jnp.concatenate(blocks, axis=1)

    def slot_points(tiles):
        wide = lanes(tiles)
        wide = wide[0:4] + wide[4:8]
        return wide[0:1], wide[1:2], wide[2:3], wide[3:4]

    u, v, _, share_slot = slot_points([points[o * 8 : (o + 1) * 8] for o in range(span)])
    land_basis = weighted_basis(share_slot, u, v)

    for i in (7, 8, 9, 10, 11, 1, 6, 14):
        loads[i].wait()
    layer_count, snow_count = layers_ref[...], snow_ref[...]
    heat = [heat_ref[z : z + 1, :] for z in range(layers)]
    start = [temp_ref[z : z + 1, :] for z in range(layers)]
    conduct = [
        jnp.where(z < snow_count, 0.25, 1.0) * cond_ref[z : z + 1, :] for z in range(layers)
    ]
    link = [
        jnp.where(
            z + 1 < layer_count,
            2.0 * conduct[z] * conduct[z + 1] / (conduct[z] + conduct[z + 1]),
            0.0,
        )
        for z in range(layers - 1)
    ]
    inverse, ratio, shift = [None] * layers, [None] * layers, [None] * layers
    for z in reversed(range(1, layers)):
        pivot = heat[z] + link[z - 1]
        right = heat[z] * start[z]
        if z + 1 < layers:
            pivot = pivot + link[z] * (1.0 - ratio[z + 1])
            right = right + link[z] * shift[z + 1]
        inverse[z] = 1.0 / pivot
        ratio[z] = link[z - 1] * inverse[z]
        shift[z] = right * inverse[z]
    base, gain = [jnp.zeros_like(heat[0])], [jnp.ones_like(heat[0])]
    for z in range(1, layers):
        base.append(shift[z] + ratio[z] * base[z - 1])
        gain.append(ratio[z] * gain[z - 1])
    shift_base, shift_gain = [None] * layers, [None] * layers
    for z in reversed(range(1, layers)):
        right_base, right_gain = heat[z] * base[z], heat[z] * gain[z]
        if z + 1 < layers:
            right_base = right_base + link[z] * shift_base[z + 1]
            right_gain = right_gain + link[z] * shift_gain[z + 1]
        shift_base[z] = right_base * inverse[z]
        shift_gain[z] = right_gain * inverse[z]
    top_pivot = heat[0] + link[0] * (1.0 - ratio[1])

    for o in coef_copies:
        coef_copies[o].wait_recv()
    got = [(coef_send if o == half else coef_recv)[o].astype(F32) for o in range(span)]
    at_points = jnp.zeros((ROWS, span * cap), F32)
    for m in range(MODES):
        at_points = at_points + land_basis[m] * lanes(
            [block[m * ROWS : (m + 1) * ROWS] for block in got]
        )
    high, low = split(at_points)
    gathered = dot(jnp.concatenate([high, low], axis=0), slot_hot[...])
    land = gathered[0:ROWS] + gathered[ROWS : 2 * ROWS]

    flux = []
    tops = []
    for s in range(SUB):
        absorbed, t_air, passed, driver = (
            land[s * FIELDS + i : s * FIELDS + i + 1] for i in range(FIELDS)
        )
        exch = 0.5 + 0.5 * driver * driver
        if s == 0:
            before, below = start[0], shift[1]
        else:
            before, below = tops[0], shift_base[1] + shift_gain[1] * tops[0]
        top = (heat[0] * before + absorbed + exch * t_air + link[0] * below) / (
            top_pivot + exch
        )
        second = below + ratio[1] * top
        tops.append(top)
        flux += [exch * (top - t_air), top, link[0] * (top - second), exch * passed]
    flux = jnp.concatenate(flux, axis=0)
    high, low = split(flux)
    spread = dot_t(jnp.concatenate([high, low], axis=0), slot_hot[...])
    spread = spread[0:ROWS] + spread[ROWS : 2 * ROWS]
    for o in range(span):
        flux_send[o] = spread[:, o * cap : (o + 1) * cap]
    flux_copies = exchange(flux_send, flux_recv, flux_sems, -1)

    excess = land_area_ref[...] - weight_sum
    partial = jnp.sum(excess * flux, axis=1, keepdims=True)
    lane = lax.broadcasted_iota(jnp.int32, (ROWS, cap), 1)
    place = lax.broadcasted_iota(jnp.int32, (ROWS, cap), 0)
    total = jnp.sum(jnp.where(lane == place, partial, 0.0), axis=0, keepdims=True)
    area = area_ref[...]
    area_total = jnp.sum(area, axis=1, keepdims=True)
    total = total + jnp.where(lane[0:1] == ROWS, area_total, 0.0)
    total_copies = []
    first = 0

    def send_total(stage, first, total):
        total_send[first] = total
        copies = []
        for i, (dr, dc) in enumerate(stage):
            copy = pltpu.make_async_remote_copy(
                src_ref=total_send.at[first],
                dst_ref=total_recv.at[first + i],
                send_sem=total_sems.at[0, first + i],
                recv_sem=total_sems.at[1, first + i],
                device_id=device(dr, dc),
                device_id_type=MESH,
            )
            copy.start()
            copies.append(copy)
        return copies

    def sum_total(stage, first, total, copies):
        for copy in copies:
            copy.wait_recv()
        for i in range(len(stage)):
            total = total + total_recv[first + i]
        return total

    pending = send_total(stages[0], 0, total)
    total_copies += pending

    rest, slope = jnp.zeros_like(heat[0]), jnp.zeros_like(heat[0])
    soil_ref[0:1, :] = tops[1]
    for z in range(1, layers):
        rest = shift_base[z] + ratio[z] * rest
        slope = shift_gain[z] + ratio[z] * slope
        soil_ref[z : z + 1, :] = rest + slope * tops[0] + gain[z] * tops[1]

    for o in point_copies:
        point_copies[o].wait_recv()
    u, v, weight_slot, _ = slot_points(
        [(point_send if o == half else point_recv)[o] for o in range(span)]
    )
    elem_basis = weighted_basis(weight_slot, u, v)
    for o in flux_copies:
        flux_copies[o].wait_recv()
    back = lanes([(flux_send if o == half else flux_recv)[o] for o in range(span)])
    terms = jnp.concatenate([elem_basis[m] * back for m in range(MODES)], axis=0)
    high, low = split(terms)
    summed = dot_t(jnp.concatenate([high, low], axis=0), elem_hot[...])
    count = MODES * ROWS
    element_coef = (summed[0:count] + summed[count : 2 * count]) / area
    high, low = split(element_coef)
    nodes = dot(basis_ref[...].astype(BF16), jnp.concatenate([high, low, high], axis=0))

    total = sum_total(stages[0], 0, total, pending)
    first = len(stages[0])
    for stage in stages[1:]:
        pending = send_total(stage, first, total)
        total_copies += pending
        total = sum_total(stage, first, total, pending)
        first += len(stage)
    spread_total = jnp.broadcast_to(total, (ROWS, cap))
    budget = jnp.sum(jnp.where(lane == place, spread_total, 0.0), axis=1, keepdims=True)
    all_area = jnp.sum(jnp.where(lane == ROWS, spread_total, 0.0), axis=1, keepdims=True)
    correction = budget / all_area
    for r in range(ROWS):
        out_ref[r // FIELDS, r % FIELDS] = (
            nodes[r * NODES : (r + 1) * NODES] + correction[r : r + 1, :]
        )

    for copies in (coef_copies, point_copies, flux_copies):
        for o in copies:
            copies[o].wait_send()
    for copy in total_copies:
        copy.wait_send()


def pass_on(nodes_ref, soil_ref, out_ref, soil_out_ref, nodes_held, soil_held, sems):
    steps = [(soil_ref, soil_held, soil_out_ref)]
    for r in range(ROWS):
        at = (r // FIELDS, r % FIELDS)
        steps.append((nodes_ref.at[at], nodes_held.at[at], out_ref.at[at]))
    reads = [
        pltpu.make_async_copy(a, b, sems.at[0, i]) for i, (a, b, _) in enumerate(steps)
    ]
    writes = [
        pltpu.make_async_copy(b, c, sems.at[1, i]) for i, (_, b, c) in enumerate(steps)
    ]
    for read in reads:
        read.start()
    for read, write in zip(reads, writes):
        read.wait()
        write.start()
    for write in writes:
        write.wait()


def local(nrows, ncols, *args):
    (
        forcing,
        elem_area,
        send_elem,
        slots,
        entry_weight,
        entry_coords,
        land_area,
        soil_temp,
        soil_cond,
        heat_cap,
        layer_count,
        snow_count,
        mix,
    ) = args
    _, span, cap = send_elem.shape
    elems = forcing.shape[3]
    cells = land_area.shape[0]
    if nrows * ncols <= 64:
        stages = [
            [(r, c) for r in range(nrows) for c in range(ncols) if (r, c) != (0, 0)]
        ]
    else:
        stages = [[(r, 0) for r in range(1, nrows)], [(0, c) for c in range(1, ncols)]]
    peers = sum(len(stage) for stage in stages)
    project, basis = block_tables()
    vmem = pl.BlockSpec(memory_space=pltpu.VMEM)
    hbm = pl.BlockSpec(memory_space=pltpu.HBM)
    operands = (
        forcing,
        elem_area.reshape(1, elems),
        send_elem.reshape(span, cap),
        slots,
        entry_weight,
        entry_coords,
        land_area.reshape(1, cells),
        soil_temp,
        soil_cond,
        heat_cap,
        layer_count.reshape(1, cells),
        snow_count.reshape(1, cells),
        mix,
        project,
        basis,
    )
    held = [
        (pltpu.SMEM if i == 12 else pltpu.VMEM)(x.shape, x.dtype)
        for i, x in enumerate(operands)
    ]
    nodes, soil = pl.pallas_call(
        functools.partial(kernel, nrows, ncols, span, cap, stages),
        out_shape=(
            jax.ShapeDtypeStruct((SUB, FIELDS, NODES, elems), F32),
            jax.ShapeDtypeStruct(soil_temp.shape, F32),
        ),
        in_specs=[hbm] * 15,
        out_specs=(vmem, vmem),
        scratch_shapes=held
        + [
            pltpu.VMEM((span, MODES * ROWS, cap), BF16),
            pltpu.VMEM((span, MODES * ROWS, cap), BF16),
            pltpu.VMEM((span, 8, cap), F32),
            pltpu.VMEM((span, 8, cap), F32),
            pltpu.VMEM((span, ROWS, cap), F32),
            pltpu.VMEM((span, ROWS, cap), F32),
            pltpu.VMEM((peers, 1, cap), F32),
            pltpu.VMEM((peers, 1, cap), F32),
            pltpu.VMEM((elems, span * cap), BF16),
            pltpu.VMEM((span * cap, cells), BF16),
            pltpu.SemaphoreType.DMA((2, span)),
            pltpu.SemaphoreType.DMA((2, span)),
            pltpu.SemaphoreType.DMA((2, span)),
            pltpu.SemaphoreType.DMA((2, peers)),
            pltpu.SemaphoreType.DMA((15,)),
        ],
        compiler_params=pltpu.CompilerParams(
            collective_id=0, has_side_effects=True, vmem_limit_bytes=60 * 1024 * 1024
        ),
    )(*operands)
    return pl.pallas_call(
        pass_on,
        out_shape=(
            jax.ShapeDtypeStruct(nodes.shape, F32),
            jax.ShapeDtypeStruct(soil.shape, F32),
        ),
        in_specs=[hbm] * 2,
        out_specs=(hbm, hbm),
        scratch_shapes=[
            pltpu.VMEM(nodes.shape, F32),
            pltpu.VMEM(soil.shape, F32),
            pltpu.SemaphoreType.DMA((2, ROWS + 1)),
        ],
        compiler_params=pltpu.CompilerParams(vmem_limit_bytes=60 * 1024 * 1024),
    )(nodes, soil)


def solution(mesh):
    placed = (
        P(None, None, None, ("row", "col")),
        P(("row", "col")),
        P("row", "col", None),
        P(None, ("row", "col")),
        P(None, ("row", "col")),
        P(None, None, ("row", "col")),
        P(("row", "col")),
        P(None, ("row", "col")),
        P(None, ("row", "col")),
        P(None, ("row", "col")),
        P(("row", "col")),
        P(("row", "col")),
        P(),
    )
    return jax.shard_map(
        functools.partial(local, mesh.shape["row"], mesh.shape["col"]),
        mesh=mesh,
        in_specs=placed,
        out_specs=(P(None, None, None, ("row", "col")), P(None, ("row", "col"))),
        check_vma=False,
    )
```
